32 devices in a mesh: grp: 2 (over x), row: 16 (over z, y, core).
Axes of the slice: x: 2, y: 2, z: 4, core: 2. Of those that a mesh axis runs over, the one named last changes fastest.
Arguments:
- geometry: float32 [9, 16384], P(None, ('grp', 'row')), parts along dimension 1, as said below
- emission: float32 [16, 16384], P(None, ('grp', 'row')), parts along dimension 1, may hold values from 0.1 to 10
- reflect: float32 [16384], P(('grp', 'row')), parts along dimension 0, may hold values from 0.2 to 0.8
- occlusion: int32 [1024, 256], P(('grp', 'row')), parts along dimension 0, may hold values from 0 to 65535
- pair_recv: int32 [1024], P(('grp', 'row')), parts along dimension 0, may hold values from 0 to 31, as said below
- pair_src: int32 [1024], P(('grp', 'row')), parts along dimension 0, may hold values from 0 to 1
- pair_count: int32 [32], P(('grp', 'row')), parts along dimension 0, may hold values from 8 to 32, as said below
Outputs:
- radiosity: float32 [16, 16384], P(None, ('grp', 'row')), parts along dimension 1
- row_sums: float32 [16384], P(('grp', 'row')), parts along dimension 0
The draws below stay inside these ranges and needn't reach their ends.
There are 2 independent parts, one for each index of `grp`. The reference program is written for one: setup_inputs(seed, part) draws one part's arguments, and reference() takes and returns one part's arrays. A program takes and returns all parts, laid end to end along the dimension named above; each array names one. Nothing has to cross between parts.
Inputs may be any that keep to these rules, and one draw needn't show every extreme that they name: `pair_recv`: in each index of row the 32 slots name distinct receiving tiles. `pair_count`: some index of row has all 32 slots live in every draw. `geometry`: edges are never parallel; every area is 0.2 or more.
All inputs are finite; a program needn't handle non-finite values.
Results may differ from the reference program's by a relative error of at most 0.0003.
Values sent between devices are 32-bit elements; how exact they have to be, the bound alone decides.
A program may use at most 64 MiB of HBM per device.

```python
import math
import jax
import jax.numpy as jnp
from jax import lax

TILE = 256
GROUPS = 16
HOURS = 16
BOUNCES = 2
TILES_DEV = 2
PAIRS_DEV = 32
TILES = 32
PATCHES = 8192
PAIRS = 512
N_ROW = 16


def draw_geometry(key, part):
    count = TILES * TILE
    keys = jax.random.split(jax.random.fold_in(key, 11), 5)
    span = 5.0
    lo_side = 0.5
    hi_side = 2.0
    box = jnp.array([span, span, span / 2.0], jnp.float32)[:, None]
    corner = jax.random.uniform(keys[0], (3, count), jnp.float32) * box
    theta = jax.random.uniform(keys[1], (count,), jnp.float32, -math.pi, math.pi)
    width = jnp.exp(jax.random.uniform(keys[2], (count,), jnp.float32, math.log(lo_side), math.log(hi_side)))
    height = jnp.exp(jax.random.uniform(keys[3], (count,), jnp.float32, math.log(lo_side), math.log(hi_side)))
    tilt = jax.random.uniform(keys[4], (2, count), jnp.float32, -1.0, 1.0)
    edge_u = jnp.stack([width * jnp.cos(theta), width * jnp.sin(theta), 0.1 * width * tilt[0]])
    edge_v = jnp.stack([0.2 * height * tilt[1], -0.2 * height * tilt[0], height])
    return jnp.concatenate([corner, edge_u, edge_v], axis=0).astype(jnp.float32)


def draw_pair_recv(key, part):
    keys = jax.random.split(jax.random.fold_in(key, 23), N_ROW)
    rows = jax.vmap(lambda k: jax.random.permutation(k, TILES)[:PAIRS_DEV])(keys)
    return rows.reshape(-1).astype(jnp.int32)


def draw_pair_count(key, part):
    base_key = jax.random.fold_in(key, 37)
    full_key = jax.random.fold_in(key, 41)
    base = jax.random.randint(base_key, (N_ROW,), PAIRS_DEV // 4, PAIRS_DEV // 2 + 1)
    full = jax.random.randint(full_key, (), 0, N_ROW)
    return jnp.where(jnp.arange(N_ROW) == full, PAIRS_DEV, base).astype(jnp.int32)


def touch_ends(values, own_key, least, top_value):
    longest = values.shape.index(max(values.shape))
    spots = []
    for shift in (0, 1):
        where = [jax.random.randint(jax.random.fold_in(own_key, axis), (), 0, length) for axis, length in enumerate(values.shape)]
        where[longest] = (where[longest] + shift) % values.shape[longest]
        spots.append(tuple(where))
    return values.at[spots[0]].set(least).at[spots[1]].set(top_value)


def level_of(key, shape, pieces, smallest, largest):
    def one(dim, shards_of):
        steps = jax.random.uniform(jax.random.fold_in(jax.random.fold_in(key, 6), dim), (shards_of,), jnp.float32, smallest / len(pieces), largest / len(pieces))
        return jnp.repeat(jnp.exp(steps), shape[dim] // shards_of).reshape((-1,) + (1,) * (len(shape) - dim - 1))

    factor_of = one(*pieces[0])
    for cut in pieces[1:]:
        factor_of = factor_of * one(*cut)
    return factor_of


def setup_inputs(seed: int = 0, part: int = 0) -> dict:
    key_list = jax.random.split(jax.random.key(seed), 8)
    part_keys = jax.random.split(jax.random.fold_in(key_list[7], part), 8)
    geometry = draw_geometry(jax.random.fold_in(jax.random.fold_in(key_list[7], part), 71), part)
    emission = jnp.clip(jnp.exp(math.log(10.0) - 4.6051702 * jax.random.uniform(part_keys[1], (HOURS, PATCHES), jnp.float32) ** level_of(part_keys[1], (HOURS, PATCHES), ((1, 16),), -0.2, 0.2)), 0.1, 10.0)
    reflect = jnp.clip(0.2 + 0.6 * jax.random.uniform(part_keys[2], (PATCHES,), jnp.float32) ** level_of(part_keys[2], (PATCHES,), ((0, 16),), -0.2, 0.2), 0.2, 0.8)
    occlusion = touch_ends(jax.random.randint(part_keys[3], (PAIRS, TILE), 0, 65536), jax.random.fold_in(part_keys[3], 1), 0, 65535).astype(jnp.int32)
    pair_recv = draw_pair_recv(jax.random.fold_in(jax.random.fold_in(key_list[7], part), 71), part)
    pair_src = touch_ends(jax.random.randint(part_keys[5], (PAIRS,), 0, TILES_DEV), jax.random.fold_in(part_keys[5], 1), 0, TILES_DEV - 1).astype(jnp.int32)
    pair_count = draw_pair_count(jax.random.fold_in(jax.random.fold_in(key_list[7], part), 71), part)
    return {"geometry": geometry, "emission": emission, "reflect": reflect, "occlusion": occlusion, "pair_recv": pair_recv, "pair_src": pair_src, "pair_count": pair_count}


def patch_frame(geometry):
    corner = geometry[0:3]
    edge_u = geometry[3:6]
    edge_v = geometry[6:9]
    cross = jnp.stack([edge_u[1] * edge_v[2] - edge_u[2] * edge_v[1], edge_u[2] * edge_v[0] - edge_u[0] * edge_v[2], edge_u[0] * edge_v[1] - edge_u[1] * edge_v[0]])
    area = jnp.sqrt(lax.optimization_barrier(jnp.sum(cross * cross, axis=0)))
    normal = cross / area
    points = jnp.stack([corner + s * edge_u + t * edge_v for s in (0.25, 0.75) for t in (0.25, 0.75)])
    return (points, normal, area)

def view_block(recv_points, recv_normal, src_points, src_normal, src_area, words, group):
    diffs = [src_points[None, :, c, None, :] - recv_points[:, None, c, :, None] for c in range(3)]
    dist_sq = diffs[0] * diffs[0] + diffs[1] * diffs[1] + diffs[2] * diffs[2]
    cos_recv = recv_normal[0][:, None] * diffs[0] + recv_normal[1][:, None] * diffs[1] + recv_normal[2][:, None] * diffs[2]
    cos_src = -(src_normal[0][None, :] * diffs[0] + src_normal[1][None, :] * diffs[1] + src_normal[2][None, :] * diffs[2])
    spread_sq = dist_sq + src_area[None, :] / 4.0
    kernel = jnp.maximum(cos_recv, 0.0) * jnp.maximum(cos_src, 0.0) / (math.pi * spread_sq * spread_sq)
    summed = lax.optimization_barrier(jnp.sum(kernel, axis=(0, 1)))
    visible = jnp.bitwise_and(jnp.right_shift(words[:, None], group[None, :]), 1).astype(jnp.float32)
    return src_area[None, :] / 16.0 * visible * summed

def reference(geometry, emission, reflect, occlusion, pair_recv, pair_src, pair_count):
    points, normal, area = patch_frame(geometry)
    tiles = TILES_DEV * N_ROW
    slots = jnp.arange(PAIRS, dtype=jnp.int32)
    owner = slots // PAIRS_DEV
    source_tile = (owner * TILES_DEV + pair_src).astype(jnp.int32)
    live = (slots % PAIRS_DEV < pair_count[owner]).astype(jnp.float32)
    group = (jnp.arange(TILE, dtype=jnp.int32) // (TILE // GROUPS)).astype(jnp.int32)

    def one_block(k):
        r_start = (pair_recv[k] * TILE).astype(jnp.int32)
        s_start = (source_tile[k] * TILE).astype(jnp.int32)
        block = view_block(lax.dynamic_slice_in_dim(points, r_start, TILE, 2), lax.dynamic_slice_in_dim(normal, r_start, TILE, 1), lax.dynamic_slice_in_dim(points, s_start, TILE, 2), lax.dynamic_slice_in_dim(normal, s_start, TILE, 1), lax.dynamic_slice_in_dim(area, s_start, TILE, 0), occlusion[k], group)
        return block * live[k]
    blocks = lax.map(one_block, slots)
    row_sums = jnp.zeros((tiles, TILE), jnp.float32).at[pair_recv].add(lax.optimization_barrier(jnp.sum(blocks, axis=2))).reshape(-1)
    scale = reflect / jnp.maximum(row_sums, 1.0)
    radiosity = emission
    for bounce in range(BOUNCES):
        source = radiosity.reshape(HOURS, tiles, TILE)[:, source_tile]
        contrib = jnp.einsum('hkj,kij->khi', source, blocks, precision=lax.Precision.HIGHEST)
        irr = jnp.zeros((tiles, HOURS, TILE), jnp.float32).at[pair_recv].add(contrib)
        irr = jnp.transpose(irr, (1, 0, 2)).reshape(HOURS, tiles * TILE)
        radiosity = emission + scale[None, :] * irr
    return (radiosity, row_sums)
```

```python
import functools
import math

import jax
import jax.numpy as jnp
from jax import lax
from jax.experimental import pallas as pl
from jax.experimental.pallas import tpu as pltpu
from jax.sharding import PartitionSpec as P

TILE = 256
GROUPS = 16
BAND = TILE // GROUPS
POINTS = 4
FEATS = 48
SPAN = (POINTS + 1) * TILE
VMEM = pl.BlockSpec(memory_space=pltpu.VMEM)
SMEM = pl.BlockSpec(memory_space=pltpu.SMEM)


def sort_kernel(recv_ref, src_ref, count_ref, occ_ref, table_ref):
    tiles = table_ref.shape[0]
    table_ref[:, :, :TILE] = jnp.zeros((tiles, 1, TILE), jnp.int32)
    table_ref[:, :, TILE:] = jnp.full((tiles, 1, 128), -1, jnp.int32)

    def place(k, carry):
        row = recv_ref[k]
        table_ref[row, :, :TILE] = occ_ref[k]
        table_ref[row, :, TILE:] = jnp.full((1, 128), src_ref[k], jnp.int32)
        return carry

    lax.fori_loop(0, count_ref[0], place, 0)


def split3(x):
    high = x.astype(jnp.bfloat16).astype(jnp.float32)
    rest = x - high
    mid = rest.astype(jnp.bfloat16).astype(jnp.float32)
    return high, mid, rest - mid


def split2(x):
    high = x.astype(jnp.bfloat16)
    return high, (x - high.astype(jnp.float32)).astype(jnp.bfloat16)


def frame(geo, center):
    corner = geo[0:3] - center
    u = geo[3:6]
    v = geo[6:9]
    ux, uy, uz = u[0:1], u[1:2], u[2:3]
    vx, vy, vz = v[0:1], v[1:2], v[2:3]
    cross = jnp.concatenate([uy * vz - uz * vy, uz * vx - ux * vz, ux * vy - uy * vx], axis=0)
    area = jnp.sqrt(jnp.sum(cross * cross, axis=0, keepdims=True))
    points = jnp.concatenate(
        [corner + s * u + t * v for s in (0.25, 0.75) for t in (0.25, 0.75)], axis=1
    )
    return points, corner, cross, area


def receiver_features(geo, center):
    points, corner, cross, area = frame(geo, center)
    normal = cross / area
    norms = jnp.sum(points * points, axis=0, keepdims=True)
    offset = -jnp.sum(normal * corner, axis=0, keepdims=True)
    wide = jnp.concatenate([-2.0 * points, normal], axis=1)
    fourth = jnp.concatenate([jnp.ones_like(norms), jnp.zeros_like(offset)], axis=1)
    fifth = jnp.concatenate([norms, offset], axis=1)
    rows = jnp.concatenate([wide, fourth, fifth, jnp.zeros((3, SPAN), jnp.float32)], axis=0)
    h, m, l = split3(rows)
    return jnp.concatenate([h, m, l, h, m, h], axis=0).astype(jnp.bfloat16)


def source_features(geo, center):
    points, corner, cross, area = frame(geo, center)
    scaled = cross * (1.0 / (16.0 * math.pi))
    norms = jnp.sum(points * points, axis=0, keepdims=True)
    spread = norms + jnp.concatenate([area * 0.25] * POINTS, axis=1)
    offset = -jnp.sum(scaled * corner, axis=0, keepdims=True)
    wide = jnp.concatenate([points, -0.5 * scaled], axis=1)
    fourth = jnp.concatenate([spread, offset], axis=1)
    fifth = jnp.concatenate([jnp.ones_like(norms), jnp.zeros_like(offset)], axis=1)
    rows = jnp.concatenate([wide, fourth, fifth, jnp.zeros((3, SPAN), jnp.float32)], axis=0)
    h, m, l = split3(rows)
    return jnp.concatenate([h, h, h, m, m, l], axis=0).T.astype(jnp.bfloat16)


def first_kernel(
    src_ref, geo_all, occ_ref, emi_all, geo_own, emi_own, refl_ref,
    blocks_ref, field_ref, sums_ref, scale_ref,
    recv_feat, src_feat, dots, facing, acc,
):
    slots = geo_all.shape[0]
    own_tiles = geo_own.shape[1] // TILE
    center = jnp.mean(geo_own[0:3, :], axis=1, keepdims=True)

    def product(p):
        return jnp.dot(
            src_feat[...],
            recv_feat[:, p * TILE : (p + 1) * TILE],
            preferred_element_type=jnp.float32,
        )

    for r in range(own_tiles):
        lanes = slice(r * TILE, (r + 1) * TILE)
        recv_feat[...] = receiver_features(geo_own[:, lanes], center)
        acc[...] = jnp.zeros_like(acc)

        def one(d, carry):
            slot = d * own_tiles + r
            src = src_ref[slot]

            @pl.when(src >= 0)
            def _():
                where = pl.ds(pl.multiple_of(src * TILE, TILE), TILE)
                src_feat[...] = source_features(geo_all[d, :, where], center)
                facing[...] = jnp.maximum(product(POINTS)[: POINTS * TILE], 0.0)
                words = occ_ref[d, r : r + 1, :TILE]
                dots[0] = product(0)
                dots[1] = product(1)
                dots[2] = product(2)
                dots[3] = product(3)
                for g in range(GROUPS):
                    total = jnp.zeros((BAND, TILE), jnp.float32)
                    for p in range(POINTS):
                        part = jnp.zeros((BAND, TILE), jnp.float32)
                        for q in range(POINTS):
                            rows = slice(q * TILE + g * BAND, q * TILE + (g + 1) * BAND)
                            spread = dots[p, rows, :]
                            part += facing[rows, :] * pl.reciprocal(spread * spread, approx=True)
                        rows = slice(POINTS * TILE + g * BAND, POINTS * TILE + (g + 1) * BAND)
                        total += jnp.maximum(dots[p, rows, :], 0.0) * part
                    bit = jnp.bitwise_and(jnp.right_shift(words, g), 1).astype(jnp.float32)
                    high, low = split2(total * bit)
                    blocks_ref[slot, g * BAND : (g + 1) * BAND, :] = high
                    blocks_ref[slot, TILE + g * BAND : TILE + (g + 1) * BAND, :] = low
                high, low = split2(emi_all[d, :, where])
                left = jnp.concatenate([high, low, jnp.ones_like(high)], axis=0)
                acc[...] += jnp.dot(
                    jnp.concatenate([left, left], axis=1),
                    blocks_ref[slot],
                    preferred_element_type=jnp.float32,
                )

            return carry

        lax.fori_loop(0, slots, one, 0)
        hours = emi_own.shape[0]
        sums = acc[2 * hours : 2 * hours + 1, :]
        irr = acc[0:hours, :] + acc[hours : 2 * hours, :]
        scale = refl_ref[:, lanes] / jnp.maximum(sums, 1.0)
        sums_ref[:, lanes] = sums
        scale_ref[:, lanes] = scale
        field_ref[:, lanes] = emi_own[:, lanes] + scale * irr


def later_kernel(src_ref, blocks_ref, field_all, emi_own, scale_ref, out_ref, acc):
    slots = field_all.shape[0]
    own_tiles = emi_own.shape[1] // TILE
    hours = emi_own.shape[0]
    for r in range(own_tiles):
        lanes = slice(r * TILE, (r + 1) * TILE)
        acc[...] = jnp.zeros_like(acc)

        def one(d, carry):
            slot = d * own_tiles + r
            src = src_ref[slot]

            @pl.when(src >= 0)
            def _():
                where = pl.ds(pl.multiple_of(src * TILE, TILE), TILE)
                high, low = split2(field_all[d, :, where])
                left = jnp.concatenate([high, low], axis=0)
                acc[...] += jnp.dot(
                    jnp.concatenate([left, left], axis=1),
                    blocks_ref[slot],
                    preferred_element_type=jnp.float32,
                )

            return carry

        lax.fori_loop(0, slots, one, 0)
        irr = acc[0:hours, :] + acc[hours : 2 * hours, :]
        out_ref[:, lanes] = emi_own[:, lanes] + scale_ref[:, lanes] * irr


def on_device(n, geometry, emission, reflect, occlusion, pair_recv, pair_src, pair_count):
    width = geometry.shape[1]
    hours = emission.shape[0]
    own_tiles = width // TILE
    tiles = own_tiles * n
    f32 = jnp.float32
    limit = pltpu.CompilerParams(vmem_limit_bytes=60 * 1024 * 1024)

    table = pl.pallas_call(
        sort_kernel,
        out_shape=jax.ShapeDtypeStruct((tiles, 1, TILE + 128), jnp.int32),
        in_specs=[SMEM, SMEM, SMEM, VMEM],
        out_specs=VMEM,
    )(pair_recv, pair_src, pair_count, occlusion[:, None, :])
    listed = lax.all_to_all(table.reshape(n, own_tiles, TILE + 128), "row", 0, 0)
    geo_all = lax.all_gather(geometry, "row", axis=0)
    emi_all = lax.all_gather(emission, "row", axis=0)
    src = listed[:, :, TILE].reshape(-1)

    blocks, field, sums, scale = pl.pallas_call(
        first_kernel,
        out_shape=(
            jax.ShapeDtypeStruct((tiles, 2 * TILE, TILE), jnp.bfloat16),
            jax.ShapeDtypeStruct((hours, width), f32),
            jax.ShapeDtypeStruct((1, width), f32),
            jax.ShapeDtypeStruct((1, width), f32),
        ),
        in_specs=[SMEM] + [VMEM] * 6,
        out_specs=(VMEM,) * 4,
        scratch_shapes=[
            pltpu.VMEM((FEATS, SPAN), jnp.bfloat16),
            pltpu.VMEM((SPAN, FEATS), jnp.bfloat16),
            pltpu.VMEM((POINTS, SPAN, TILE), f32),
            pltpu.VMEM((POINTS * TILE, TILE), f32),
            pltpu.VMEM((3 * hours, TILE), f32),
        ],
        compiler_params=limit,
    )(src, geo_all, listed, emi_all, geometry, emission, reflect.reshape(1, width))

    field_all = lax.all_gather(field, "row", axis=0)
    radiosity = pl.pallas_call(
        later_kernel,
        out_shape=jax.ShapeDtypeStruct((hours, width), f32),
        in_specs=[SMEM] + [VMEM] * 4,
        out_specs=VMEM,
        scratch_shapes=[pltpu.VMEM((2 * hours, TILE), f32)],
        compiler_params=limit,
    )(src, blocks, field_all, emission, scale)
    return (radiosity, sums.reshape(width))


def solution(mesh):
    placed = (
        P(None, ("grp", "row")),
        P(None, ("grp", "row")),
        P(("grp", "row")),
        P(("grp", "row"), None),
        P(("grp", "row")),
        P(("grp", "row")),
        P(("grp", "row")),
    )
    return jax.shard_map(
        functools.partial(on_device, mesh.shape["row"]),
        mesh=mesh,
        in_specs=placed,
        out_specs=(P(None, ("grp", "row")), P(("grp", "row"))),
        check_vma=False,
    )
```

```python
import functools
import math

import jax
import jax.numpy as jnp
from jax import lax
from jax.experimental import pallas as pl
from jax.experimental.pallas import tpu as pltpu
from jax.sharding import PartitionSpec as P

TILE = 256
GROUPS = 16
BAND = TILE // GROUPS
POINTS = 4
FEATS = 48
PACK = 32
SPAN = (POINTS + 1) * TILE
VMEM = pl.BlockSpec(memory_space=pltpu.VMEM)
SMEM = pl.BlockSpec(memory_space=pltpu.SMEM)


def sort_kernel(recv_ref, src_ref, count_ref, occ_ref, table_ref):
    tiles = table_ref.shape[0]
    table_ref[:, :, :TILE] = jnp.zeros((tiles, 1, TILE), jnp.int32)
    table_ref[:, :, TILE:] = jnp.full((tiles, 1, 128), -1, jnp.int32)

    def place(k, carry):
        row = recv_ref[k]
        table_ref[row, :, :TILE] = occ_ref[pl.ds(k, 1), :]
        table_ref[row, :, TILE:] = jnp.full((1, 128), src_ref[k], jnp.int32)
        return carry

    lax.fori_loop(0, count_ref[0], place, 0)


def start_gather(n, own, out, send, recv):
    me = lax.axis_index("row")
    depth = n // 4
    core = lax.rem(me, 2)
    side = lax.rem(me // 2, 2)
    level = me // 4

    def index(a, b, c):
        return a * 4 + b * 2 + c

    def copy(source, slot, device, k):
        return pltpu.make_async_remote_copy(
            src_ref=source,
            dst_ref=out.at[slot],
            send_sem=send.at[k],
            recv_sem=recv.at[slot],
            device_id={"row": device},
            device_id_type=pl.DeviceIdType.MESH,
        )

    across = index(level, 1 - side, core)
    partner = index(level, side, 1 - core)
    started = []

    def begin(source, slot, device):
        made = copy(source, slot, device, len(started))
        made.start()
        started.append(made)

    for step in range(1, depth):
        begin(own, me, index(lax.rem(level + step, depth), side, core))
    begin(own, me, across)
    begin(own, me, partner)

    def arrived(slot):
        copy(out.at[slot], slot, partner, 0).wait_recv()

    def finish():
        for step in range(1, depth):
            slot = index(lax.rem(level - step + depth, depth), side, core)
            arrived(slot)
            begin(out.at[slot], slot, across)
            begin(out.at[slot], slot, partner)
        for step in range(depth):
            slot = index(lax.rem(level - step + depth, depth), 1 - side, core)
            arrived(slot)
            begin(out.at[slot], slot, partner)
        for step in range(depth):
            for b in range(2):
                arrived(index(lax.rem(level - step + depth, depth), b, 1 - core))
        for made in started:
            made.wait_send()

    return finish


def sends(n):
    depth = n // 4
    return 3 * depth - 1 + 2 * depth


def greet(n):
    me = lax.axis_index("row")
    barrier = pltpu.get_barrier_semaphore()
    for step in range(1, n):
        pl.semaphore_signal(
            barrier,
            inc=1,
            device_id={"row": lax.rem(me + step, n)},
            device_id_type=pl.DeviceIdType.MESH,
        )
    pl.semaphore_wait(barrier, n - 1)


def share_kernel(n, emi_ref, geo_ref, table_ref, out_ref, listed_ref, send, recv, list_send, list_recv):
    me = lax.axis_index("row")
    hours = emi_ref.shape[0]
    own_tiles = table_ref.shape[0] // n
    out_ref[me, :hours] = emi_ref[...]
    out_ref[me, hours : hours + 9] = geo_ref[...]
    out_ref[me, hours + 9 :] = jnp.zeros_like(out_ref[me, hours + 9 :])
    listed_ref[me] = table_ref[pl.ds(me * own_tiles, own_tiles)]
    greet(n)
    finish = start_gather(n, out_ref.at[me], out_ref, send, recv)
    lists = []
    for step in range(1, n):
        device = lax.rem(me + step, n)
        made = pltpu.make_async_remote_copy(
            src_ref=table_ref.at[pl.ds(device * own_tiles, own_tiles)],
            dst_ref=listed_ref.at[me],
            send_sem=list_send.at[step],
            recv_sem=list_recv.at[step],
            device_id={"row": device},
            device_id_type=pl.DeviceIdType.MESH,
        )
        made.start()
        lists.append(made)
    finish()
    for made in lists:
        made.wait()


def field_kernel(n, field_ref, out_ref, send, recv):
    me = lax.axis_index("row")
    out_ref[me] = field_ref[...]
    greet(n)
    start_gather(n, field_ref, out_ref, send, recv)()


def split3(x):
    high = x.astype(jnp.bfloat16).astype(jnp.float32)
    rest = x - high
    mid = rest.astype(jnp.bfloat16).astype(jnp.float32)
    return high, mid, rest - mid


def split2(x):
    high = x.astype(jnp.bfloat16)
    return high, (x - high.astype(jnp.float32)).astype(jnp.bfloat16)


def frame(geo, center):
    corner = geo[0:3] - center
    u = geo[3:6]
    v = geo[6:9]
    ux, uy, uz = u[0:1], u[1:2], u[2:3]
    vx, vy, vz = v[0:1], v[1:2], v[2:3]
    cross = jnp.concatenate([uy * vz - uz * vy, uz * vx - ux * vz, ux * vy - uy * vx], axis=0)
    area = jnp.sqrt(jnp.sum(cross * cross, axis=0, keepdims=True))
    points = jnp.concatenate(
        [corner + s * u + t * v for s in (0.25, 0.75) for t in (0.25, 0.75)], axis=1
    )
    return points, corner, cross, area


def receiver_features(geo, center):
    points, corner, cross, area = frame(geo, center)
    normal = cross / area
    norms = jnp.sum(points * points, axis=0, keepdims=True)
    offset = -jnp.sum(normal * corner, axis=0, keepdims=True)
    wide = jnp.concatenate([-2.0 * points, normal], axis=1)
    fourth = jnp.concatenate([jnp.ones_like(norms), jnp.zeros_like(offset)], axis=1)
    fifth = jnp.concatenate([norms, offset], axis=1)
    rows = jnp.concatenate([wide, fourth, fifth, jnp.zeros((3, SPAN), jnp.float32)], axis=0)
    h, m, l = split3(rows)
    return jnp.concatenate([h, m, l, h, m, h], axis=0).astype(jnp.bfloat16)


def source_features(geo, center):
    points, corner, cross, area = frame(geo, center)
    scaled = cross * (1.0 / (16.0 * math.pi))
    norms = jnp.sum(points * points, axis=0, keepdims=True)
    spread = norms + jnp.concatenate([area * 0.25] * POINTS, axis=1)
    offset = -jnp.sum(scaled * corner, axis=0, keepdims=True)
    wide = jnp.concatenate([points, -0.5 * scaled], axis=1)
    fourth = jnp.concatenate([spread, offset], axis=1)
    fifth = jnp.concatenate([jnp.ones_like(norms), jnp.zeros_like(offset)], axis=1)
    rows = jnp.concatenate([wide, fourth, fifth, jnp.zeros((3, SPAN), jnp.float32)], axis=0)
    h, m, l = split3(rows)
    return jnp.concatenate([h, h, h, m, m, l], axis=0).T.astype(jnp.bfloat16)


def first_kernel(
    src_ref, packed, occ_ref, geo_own, emi_own, refl_ref,
    blocks_ref, field_ref, sums_ref, scale_ref,
    recv_feat, src_feat, dots, facing, acc,
):
    slots = packed.shape[0]
    hours = emi_own.shape[0]
    own_tiles = geo_own.shape[1] // TILE
    center = jnp.mean(geo_own[0:3, :], axis=1, keepdims=True)

    def product(p):
        return jnp.dot(
            src_feat[...],
            recv_feat[:, p * TILE : (p + 1) * TILE],
            preferred_element_type=jnp.float32,
        )

    for r in range(own_tiles):
        lanes = slice(r * TILE, (r + 1) * TILE)
        recv_feat[...] = receiver_features(geo_own[:, lanes], center)
        acc[...] = jnp.zeros_like(acc)

        def one(d, carry):
            slot = d * own_tiles + r
            src = src_ref[slot]

            @pl.when(src >= 0)
            def _():
                where = pl.ds(pl.multiple_of(src * TILE, TILE), TILE)
                src_feat[...] = source_features(packed[d, hours : hours + 9, where], center)
                facing[...] = jnp.maximum(product(POINTS)[: POINTS * TILE], 0.0)
                words = occ_ref[d, r, :, :TILE]
                dots[0] = product(0)
                dots[1] = product(1)
                dots[2] = product(2)
                dots[3] = product(3)
                for g in range(GROUPS):
                    total = jnp.zeros((BAND, TILE), jnp.float32)
                    for p in range(POINTS):
                        part = jnp.zeros((BAND, TILE), jnp.float32)
                        for q in range(POINTS):
                            rows = slice(q * TILE + g * BAND, q * TILE + (g + 1) * BAND)
                            spread = dots[p, rows, :]
                            part += facing[rows, :] * pl.reciprocal(spread * spread, approx=True)
                        rows = slice(POINTS * TILE + g * BAND, POINTS * TILE + (g + 1) * BAND)
                        total += jnp.maximum(dots[p, rows, :], 0.0) * part
                    bit = jnp.bitwise_and(jnp.right_shift(words, g), 1).astype(jnp.float32)
                    high, low = split2(total * bit)
                    blocks_ref[slot, g * BAND : (g + 1) * BAND, :] = high
                    blocks_ref[slot, TILE + g * BAND : TILE + (g + 1) * BAND, :] = low
                high, low = split2(packed[d, :hours, where])
                left = jnp.concatenate([high, low, jnp.ones_like(high)], axis=0)
                acc[...] += jnp.dot(
                    jnp.concatenate([left, left], axis=1),
                    blocks_ref[slot],
                    preferred_element_type=jnp.float32,
                )

            return carry

        lax.fori_loop(0, slots, one, 0)
        sums = acc[2 * hours : 2 * hours + 1, :]
        irr = acc[0:hours, :] + acc[hours : 2 * hours, :]
        scale = refl_ref[:, lanes] / jnp.maximum(sums, 1.0)
        sums_ref[:, lanes] = sums
        scale_ref[:, lanes] = scale
        field_ref[:, lanes] = emi_own[:, lanes] + scale * irr


def later_kernel(src_ref, blocks_ref, field_all, emi_own, scale_ref, out_ref, acc):
    slots = field_all.shape[0]
    own_tiles = emi_own.shape[1] // TILE
    hours = emi_own.shape[0]
    for r in range(own_tiles):
        lanes = slice(r * TILE, (r + 1) * TILE)
        acc[...] = jnp.zeros_like(acc)

        def one(d, carry):
            slot = d * own_tiles + r
            src = src_ref[slot]

            @pl.when(src >= 0)
            def _():
                where = pl.ds(pl.multiple_of(src * TILE, TILE), TILE)
                high, low = split2(field_all[d, :, where])
                left = jnp.concatenate([high, low], axis=0)
                acc[...] += jnp.dot(
                    jnp.concatenate([left, left], axis=1),
                    blocks_ref[slot],
                    preferred_element_type=jnp.float32,
                )

            return carry

        lax.fori_loop(0, slots, one, 0)
        irr = acc[0:hours, :] + acc[hours : 2 * hours, :]
        out_ref[:, lanes] = emi_own[:, lanes] + scale_ref[:, lanes] * irr


def on_device(n, geometry, emission, reflect, occlusion, pair_recv, pair_src, pair_count):
    width = geometry.shape[1]
    hours = emission.shape[0]
    own_tiles = width // TILE
    tiles = own_tiles * n
    f32 = jnp.float32
    limit = pltpu.CompilerParams(vmem_limit_bytes=60 * 1024 * 1024)

    table = pl.pallas_call(
        sort_kernel,
        out_shape=jax.ShapeDtypeStruct((tiles, 1, TILE + 128), jnp.int32),
        in_specs=[SMEM, SMEM, SMEM, VMEM],
        out_specs=VMEM,
    )(pair_recv, pair_src, pair_count, occlusion)
    dma = pltpu.SemaphoreType.DMA
    packed, listed = pl.pallas_call(
        functools.partial(share_kernel, n),
        out_shape=(
            jax.ShapeDtypeStruct((n, PACK, width), f32),
            jax.ShapeDtypeStruct((n, own_tiles, 1, TILE + 128), jnp.int32),
        ),
        in_specs=[VMEM] * 3,
        out_specs=(VMEM,) * 2,
        scratch_shapes=[dma((sends(n),)), dma((n,)), dma((n,)), dma((n,))],
        compiler_params=pltpu.CompilerParams(
            collective_id=0, has_side_effects=True, vmem_limit_bytes=60 * 1024 * 1024
        ),
    )(emission, geometry, table)
    src = listed[:, :, 0, TILE].reshape(-1)

    blocks, field, sums, scale = pl.pallas_call(
        first_kernel,
        out_shape=(
            jax.ShapeDtypeStruct((tiles, 2 * TILE, TILE), jnp.bfloat16),
            jax.ShapeDtypeStruct((hours, width), f32),
            jax.ShapeDtypeStruct((1, width), f32),
            jax.ShapeDtypeStruct((1, width), f32),
        ),
        in_specs=[SMEM] + [VMEM] * 5,
        out_specs=(VMEM,) * 4,
        scratch_shapes=[
            pltpu.VMEM((FEATS, SPAN), jnp.bfloat16),
            pltpu.VMEM((SPAN, FEATS), jnp.bfloat16),
            pltpu.VMEM((POINTS, SPAN, TILE), f32),
            pltpu.VMEM((POINTS * TILE, TILE), f32),
            pltpu.VMEM((3 * hours, TILE), f32),
        ],
        compiler_params=limit,
    )(src, packed, listed, geometry, emission, reflect.reshape(1, width))

    field_all = pl.pallas_call(
        functools.partial(field_kernel, n),
        out_shape=jax.ShapeDtypeStruct((n, hours, width), f32),
        in_specs=[VMEM],
        out_specs=VMEM,
        scratch_shapes=[dma((sends(n),)), dma((n,))],
        compiler_params=pltpu.CompilerParams(
            collective_id=1, has_side_effects=True, vmem_limit_bytes=60 * 1024 * 1024
        ),
    )(field)
    radiosity = pl.pallas_call(
        later_kernel,
        out_shape=jax.ShapeDtypeStruct((hours, width), f32),
        in_specs=[SMEM] + [VMEM] * 4,
        out_specs=VMEM,
        scratch_shapes=[pltpu.VMEM((2 * hours, TILE), f32)],
        compiler_params=limit,
    )(src, blocks, field_all, emission, scale)
    return (radiosity, sums.reshape(width))


def solution(mesh):
    placed = (
        P(None, ("grp", "row")),
        P(None, ("grp", "row")),
        P(("grp", "row")),
        P(("grp", "row"), None),
        P(("grp", "row")),
        P(("grp", "row")),
        P(("grp", "row")),
    )
    return jax.shard_map(
        functools.partial(on_device, mesh.shape["row"]),
        mesh=mesh,
        in_specs=placed,
        out_specs=(P(None, ("grp", "row")), P(("grp", "row"))),
        check_vma=False,
    )
```

```python
import functools
import math

import jax
import jax.numpy as jnp
from jax import lax
from jax.experimental import pallas as pl
from jax.experimental.pallas import tpu as pltpu
from jax.sharding import PartitionSpec as P

TILE = 256
GROUPS = 16
BAND = TILE // GROUPS
POINTS = 4
FEATS = 48
PACK = 32
CHUNKS = 4
PART = TILE // CHUNKS
SPAN = (POINTS + 1) * TILE
VMEM = pl.BlockSpec(memory_space=pltpu.VMEM)
SMEM = pl.BlockSpec(memory_space=pltpu.SMEM)


def sort_kernel(recv_ref, src_ref, count_ref, occ_ref, table_ref):
    tiles = table_ref.shape[0]
    table_ref[:, :, :TILE] = jnp.zeros((tiles, 1, TILE), jnp.int32)
    table_ref[:, :, TILE:] = jnp.full((tiles, 1, 128), -1, jnp.int32)

    def place(k, carry):
        row = recv_ref[k]
        table_ref[row, :, :TILE] = occ_ref[pl.ds(k, 1), :]
        table_ref[row, :, TILE:] = jnp.full((1, 128), src_ref[k], jnp.int32)
        return carry

    lax.fori_loop(0, count_ref[0], place, 0)


def start_gather(n, own, out, send, recv):
    me = lax.axis_index("row")
    depth = n // 4
    core = lax.rem(me, 2)
    side = lax.rem(me // 2, 2)
    level = me // 4

    def index(a, b, c):
        return a * 4 + b * 2 + c

    def copy(source, slot, device, k):
        return pltpu.make_async_remote_copy(
            src_ref=source,
            dst_ref=out.at[slot],
            send_sem=send.at[k],
            recv_sem=recv.at[slot],
            device_id={"row": device},
            device_id_type=pl.DeviceIdType.MESH,
        )

    across = index(level, 1 - side, core)
    partner = index(level, side, 1 - core)
    started = []

    def begin(source, slot, device):
        made = copy(source, slot, device, len(started))
        made.start()
        started.append(made)

    for step in range(1, depth):
        begin(own, me, index(lax.rem(level + step, depth), side, core))
    begin(own, me, across)
    begin(own, me, partner)

    def arrived(slot):
        copy(out.at[slot], slot, partner, 0).wait_recv()

    def finish():
        for step in range(1, depth):
            slot = index(lax.rem(level - step + depth, depth), side, core)
            arrived(slot)
            begin(out.at[slot], slot, across)
            begin(out.at[slot], slot, partner)
        for step in range(depth):
            slot = index(lax.rem(level - step + depth, depth), 1 - side, core)
            arrived(slot)
            begin(out.at[slot], slot, partner)
        for step in range(depth):
            for b in range(2):
                arrived(index(lax.rem(level - step + depth, depth), b, 1 - core))
        for made in started:
            made.wait_send()

    return finish


def sends(n):
    depth = n // 4
    return 3 * depth - 1 + 2 * depth


def greet(n):
    me = lax.axis_index("row")
    barrier = pltpu.get_barrier_semaphore()
    for step in range(1, n):
        pl.semaphore_signal(
            barrier,
            inc=1,
            device_id={"row": lax.rem(me + step, n)},
            device_id_type=pl.DeviceIdType.MESH,
        )
    pl.semaphore_wait(barrier, n - 1)


def share_kernel(n, emi_ref, geo_ref, table_ref, out_ref, listed_ref, codes_ref, send, recv, list_send, list_recv):
    me = lax.axis_index("row")
    hours = emi_ref.shape[0]
    own_tiles = table_ref.shape[0] // n
    out_ref[me, :hours] = emi_ref[...]
    out_ref[me, hours : hours + 9] = geo_ref[...]
    out_ref[me, hours + 9 :] = jnp.zeros_like(out_ref[me, hours + 9 :])
    listed_ref[me] = table_ref[pl.ds(me * own_tiles, own_tiles)]
    greet(n)
    finish = start_gather(n, out_ref.at[me], out_ref, send, recv)
    lists = []
    for step in range(1, n):
        device = lax.rem(me + step, n)
        made = pltpu.make_async_remote_copy(
            src_ref=table_ref.at[pl.ds(device * own_tiles, own_tiles)],
            dst_ref=listed_ref.at[me],
            send_sem=list_send.at[step],
            recv_sem=list_recv.at[step],
            device_id={"row": device},
            device_id_type=pl.DeviceIdType.MESH,
        )
        made.start()
        lists.append(made)
    finish()
    for made in lists:
        made.wait()
    for d in range(n):
        codes_ref[d * own_tiles : (d + 1) * own_tiles, :] = listed_ref[d, :, 0, TILE:]


def field_kernel(n, field_ref, out_ref, send, recv):
    me = lax.axis_index("row")
    out_ref[me] = field_ref[...]
    greet(n)
    start_gather(n, field_ref, out_ref, send, recv)()


def split3(x):
    high = x.astype(jnp.bfloat16).astype(jnp.float32)
    rest = x - high
    mid = rest.astype(jnp.bfloat16).astype(jnp.float32)
    return high, mid, rest - mid


def split2(x):
    high = x.astype(jnp.bfloat16)
    return high, (x - high.astype(jnp.float32)).astype(jnp.bfloat16)


def frame(geo, center):
    corner = geo[0:3] - center
    u = geo[3:6]
    v = geo[6:9]
    ux, uy, uz = u[0:1], u[1:2], u[2:3]
    vx, vy, vz = v[0:1], v[1:2], v[2:3]
    cross = jnp.concatenate([uy * vz - uz * vy, uz * vx - ux * vz, ux * vy - uy * vx], axis=0)
    area = jnp.sqrt(jnp.sum(cross * cross, axis=0, keepdims=True))
    points = jnp.concatenate(
        [corner + s * u + t * v for s in (0.25, 0.75) for t in (0.25, 0.75)], axis=1
    )
    return points, corner, cross, area


def receiver_features(geo, center):
    points, corner, cross, area = frame(geo, center)
    normal = cross / area
    norms = jnp.sum(points * points, axis=0, keepdims=True)
    offset = -jnp.sum(normal * corner, axis=0, keepdims=True)
    wide = jnp.concatenate([-2.0 * points, normal], axis=1)
    fourth = jnp.concatenate([jnp.ones_like(norms), jnp.zeros_like(offset)], axis=1)
    fifth = jnp.concatenate([norms, offset], axis=1)
    rows = jnp.concatenate([wide, fourth, fifth, jnp.zeros((3, SPAN), jnp.float32)], axis=0)
    h, m, l = split3(rows)
    return jnp.concatenate([h, m, l, h, m, h], axis=0).astype(jnp.bfloat16)


def source_features(geo, center):
    points, corner, cross, area = frame(geo, center)
    scaled = cross * (1.0 / (16.0 * math.pi))
    norms = jnp.sum(points * points, axis=0, keepdims=True)
    spread = norms + jnp.concatenate([area * 0.25] * POINTS, axis=1)
    offset = -jnp.sum(scaled * corner, axis=0, keepdims=True)
    wide = jnp.concatenate([points, -0.5 * scaled], axis=1)
    fourth = jnp.concatenate([spread, offset], axis=1)
    fifth = jnp.concatenate([jnp.ones_like(norms), jnp.zeros_like(offset)], axis=1)
    rows = jnp.concatenate([wide, fourth, fifth, jnp.zeros((3, SPAN), jnp.float32)], axis=0)
    h, m, l = split3(rows)
    return jnp.concatenate([h, h, h, m, m, l], axis=0).T.astype(jnp.bfloat16)


def first_kernel(
    src_ref, packed, occ_ref, geo_own, emi_own, refl_ref,
    blocks_ref, field_ref, sums_ref, scale_ref,
    order, recv_feat, src_feat, dots, facing, total, acc,
):
    own_tiles = geo_own.shape[1] // TILE
    slots = packed.shape[0] * own_tiles
    hours = emi_own.shape[0]
    center = jnp.mean(geo_own[0:3, :], axis=1, keepdims=True)

    def listing(k, live):
        order[live] = k
        return live + jnp.where(src_ref[k, 0] >= 0, 1, 0)

    count = lax.fori_loop(0, slots, listing, 0)
    for r in range(own_tiles):
        recv_feat[r] = receiver_features(geo_own[:, r * TILE : (r + 1) * TILE], center)
    acc[...] = jnp.zeros_like(acc)

    def place(slot):
        src = jnp.maximum(src_ref[slot, 0], 0)
        return slot // own_tiles, pl.ds(pl.multiple_of(src * TILE, TILE), TILE)

    def load_features(slot):
        d, where = place(slot)
        rows = source_features(packed[d, hours : hours + 9, where], center)
        for c in range(CHUNKS):
            for q in range(POINTS):
                src_feat[c * TILE + q * PART : c * TILE + (q + 1) * PART, :] = rows[
                    q * TILE + c * PART : q * TILE + (c + 1) * PART
                ]
        src_feat[POINTS * TILE :, :] = rows[POINTS * TILE :]

    def product(r, piece, p):
        return jnp.dot(
            src_feat[piece * TILE : (piece + 1) * TILE, :],
            recv_feat[r, :, p * TILE : (p + 1) * TILE],
            preferred_element_type=jnp.float32,
        )

    def face(r, c):
        facing[c * TILE : (c + 1) * TILE, :] = jnp.maximum(product(r, c, POINTS), 0.0)

    def fill(r, c, p):
        dots[p % 2, c * TILE : (c + 1) * TILE, :] = product(r, c, p)

    def combine(p, c, finish):
        for b in range(PART // BAND):
            inner = b * BAND
            part = jnp.zeros((BAND, TILE), jnp.float32)
            for q in range(POINTS):
                row = c * TILE + q * PART + inner
                spread = dots[p % 2, row : row + BAND, :]
                inverse = pl.reciprocal(spread * spread, approx=True)
                part += facing[row : row + BAND, :] * inverse
            row = c * PART + inner
            back = dots[p % 2, POINTS * TILE + row : POINTS * TILE + row + BAND, :]
            value = jnp.maximum(back, 0.0) * part
            if p > 0:
                value += total[row : row + BAND, :]
            if p < POINTS - 1:
                total[row : row + BAND, :] = value
            else:
                finish(row, value)

    def prepare(slot):
        load_features(slot)
        r = lax.rem(slot, own_tiles)
        fill(r, CHUNKS, 0)
        for c in range(CHUNKS):
            face(r, c)
            fill(r, c, 0)

    prepare(order[0])

    def one(i, carry):
        slot = order[i]
        later = order[jnp.minimum(i + 1, count - 1)]
        r = lax.rem(slot, own_tiles)
        later_r = lax.rem(later, own_tiles)
        d, where = place(slot)
        words = occ_ref[d, r, :, :TILE]

        def finish(row, value):
            bit = jnp.bitwise_and(jnp.right_shift(words, row // BAND), 1).astype(jnp.float32)
            high, low = split2(value * bit)
            blocks_ref[slot, row : row + BAND, :] = high
            blocks_ref[slot, TILE + row : TILE + row + BAND, :] = low

        for p in range(POINTS - 1):
            fill(r, CHUNKS, p + 1)
            for c in range(CHUNKS):
                fill(r, c, p + 1)
                combine(p, c, finish)
        load_features(later)
        fill(later_r, CHUNKS, 0)
        for c in range(CHUNKS):
            combine(POINTS - 1, c, finish)
            face(later_r, c)
            fill(later_r, c, 0)
        high, low = split2(packed[d, :hours, where])
        left = jnp.concatenate([high, low, jnp.ones_like(high)], axis=0)
        acc[r] += jnp.dot(
            jnp.concatenate([left, left], axis=1),
            blocks_ref[slot],
            preferred_element_type=jnp.float32,
        )
        return carry

    lax.fori_loop(0, count, one, 0)
    for r in range(own_tiles):
        lanes = slice(r * TILE, (r + 1) * TILE)
        sums = acc[r, 2 * hours : 2 * hours + 1, :]
        irr = acc[r, 0:hours, :] + acc[r, hours : 2 * hours, :]
        scale = refl_ref[:, lanes] / jnp.maximum(sums, 1.0)
        sums_ref[:, lanes] = sums
        scale_ref[:, lanes] = scale
        field_ref[:, lanes] = emi_own[:, lanes] + scale * irr


def later_kernel(src_ref, blocks_ref, field_all, emi_own, scale_ref, out_ref, acc):
    slots = field_all.shape[0]
    own_tiles = emi_own.shape[1] // TILE
    hours = emi_own.shape[0]
    for r in range(own_tiles):
        lanes = slice(r * TILE, (r + 1) * TILE)
        acc[...] = jnp.zeros_like(acc)

        def one(d, carry):
            slot = d * own_tiles + r
            src = src_ref[slot, 0]

            @pl.when(src >= 0)
            def _():
                where = pl.ds(pl.multiple_of(src * TILE, TILE), TILE)
                high, low = split2(field_all[d, :, where])
                left = jnp.concatenate([high, low], axis=0)
                acc[...] += jnp.dot(
                    jnp.concatenate([left, left], axis=1),
                    blocks_ref[slot],
                    preferred_element_type=jnp.float32,
                )

            return carry

        lax.fori_loop(0, slots, one, 0)
        irr = acc[0:hours, :] + acc[hours : 2 * hours, :]
        out_ref[:, lanes] = emi_own[:, lanes] + scale_ref[:, lanes] * irr


def on_device(n, geometry, emission, reflect, occlusion, pair_recv, pair_src, pair_count):
    width = geometry.shape[1]
    hours = emission.shape[0]
    own_tiles = width // TILE
    tiles = own_tiles * n
    f32 = jnp.float32
    limit = pltpu.CompilerParams(vmem_limit_bytes=60 * 1024 * 1024)

    table = pl.pallas_call(
        sort_kernel,
        out_shape=jax.ShapeDtypeStruct((tiles, 1, TILE + 128), jnp.int32),
        in_specs=[SMEM, SMEM, SMEM, VMEM],
        out_specs=VMEM,
    )(pair_recv, pair_src, pair_count, occlusion)
    dma = pltpu.SemaphoreType.DMA
    packed, listed, codes = pl.pallas_call(
        functools.partial(share_kernel, n),
        out_shape=(
            jax.ShapeDtypeStruct((n, PACK, width), f32),
            jax.ShapeDtypeStruct((n, own_tiles, 1, TILE + 128), jnp.int32),
            jax.ShapeDtypeStruct((tiles, 128), jnp.int32),
        ),
        in_specs=[VMEM] * 3,
        out_specs=(VMEM,) * 3,
        scratch_shapes=[dma((sends(n),)), dma((n,)), dma((n,)), dma((n,))],
        compiler_params=pltpu.CompilerParams(
            collective_id=0, has_side_effects=True, vmem_limit_bytes=60 * 1024 * 1024
        ),
    )(emission, geometry, table)

    blocks, field, sums, scale = pl.pallas_call(
        first_kernel,
        out_shape=(
            jax.ShapeDtypeStruct((tiles, 2 * TILE, TILE), jnp.bfloat16),
            jax.ShapeDtypeStruct((hours, width), f32),
            jax.ShapeDtypeStruct((1, width), f32),
            jax.ShapeDtypeStruct((1, width), f32),
        ),
        in_specs=[SMEM] + [VMEM] * 5,
        out_specs=(VMEM,) * 4,
        scratch_shapes=[
            pltpu.SMEM((tiles,), jnp.int32),
            pltpu.VMEM((own_tiles, FEATS, SPAN), jnp.bfloat16),
            pltpu.VMEM((SPAN, FEATS), jnp.bfloat16),
            pltpu.VMEM((2, SPAN, TILE), f32),
            pltpu.VMEM((POINTS * TILE, TILE), f32),
            pltpu.VMEM((TILE, TILE), f32),
            pltpu.VMEM((own_tiles, 3 * hours, TILE), f32),
        ],
        compiler_params=limit,
    )(codes, packed, listed, geometry, emission, reflect.reshape(1, width))

    field_all = pl.pallas_call(
        functools.partial(field_kernel, n),
        out_shape=jax.ShapeDtypeStruct((n, hours, width), f32),
        in_specs=[VMEM],
        out_specs=VMEM,
        scratch_shapes=[dma((sends(n),)), dma((n,))],
        compiler_params=pltpu.CompilerParams(
            collective_id=1, has_side_effects=True, vmem_limit_bytes=60 * 1024 * 1024
        ),
    )(field)
    radiosity = pl.pallas_call(
        later_kernel,
        out_shape=jax.ShapeDtypeStruct((hours, width), f32),
        in_specs=[SMEM] + [VMEM] * 4,
        out_specs=VMEM,
        scratch_shapes=[pltpu.VMEM((2 * hours, TILE), f32)],
        compiler_params=limit,
    )(codes, blocks, field_all, emission, scale)
    return (radiosity, sums.reshape(width))


def solution(mesh):
    placed = (
        P(None, ("grp", "row")),
        P(None, ("grp", "row")),
        P(("grp", "row")),
        P(("grp", "row"), None),
        P(("grp", "row")),
        P(("grp", "row")),
        P(("grp", "row")),
    )
    return jax.shard_map(
        functools.partial(on_device, mesh.shape["row"]),
        mesh=mesh,
        in_specs=placed,
        out_specs=(P(None, ("grp", "row")), P(("grp", "row"))),
        check_vma=False,
    )
```

```python
import functools
import math

import jax
import jax.numpy as jnp
from jax import lax
from jax.experimental import pallas as pl
from jax.experimental.pallas import tpu as pltpu
from jax.sharding import PartitionSpec as P

TILE = 256
GROUPS = 16
BAND = TILE // GROUPS
POINTS = 4
FEATS = 48
PACK = 32
CHUNKS = 4
PART = TILE // CHUNKS
WIDE = 2 * TILE
SPAN = (POINTS + 1) * TILE
VMEM = pl.BlockSpec(memory_space=pltpu.VMEM)
ANY = pl.BlockSpec(memory_space=pl.ANY)
SMEM = pl.BlockSpec(memory_space=pltpu.SMEM)


def sort_kernel(recv_ref, src_ref, count_ref, occ_ref, table_ref):
    tiles = table_ref.shape[0]
    table_ref[:, :, :TILE] = jnp.zeros((tiles, 1, TILE), jnp.int32)
    table_ref[:, :, TILE:] = jnp.full((tiles, 1, 128), -1, jnp.int32)

    def place(k, carry):
        row = recv_ref[k]
        table_ref[row, :, :TILE] = occ_ref[pl.ds(k, 1), :]
        table_ref[row, :, TILE:] = jnp.full((1, 128), src_ref[k], jnp.int32)
        return carry

    lax.fori_loop(0, count_ref[0], place, 0)


def start_gather(n, own, out, send, recv):
    me = lax.axis_index("row")
    depth = n // 4
    core = lax.rem(me, 2)
    side = lax.rem(me // 2, 2)
    level = me // 4

    def index(a, b, c):
        return a * 4 + b * 2 + c

    def copy(source, slot, device, k):
        return pltpu.make_async_remote_copy(
            src_ref=source,
            dst_ref=out.at[slot],
            send_sem=send.at[k],
            recv_sem=recv.at[slot],
            device_id={"row": device},
            device_id_type=pl.DeviceIdType.MESH,
        )

    across = index(level, 1 - side, core)
    partner = index(level, side, 1 - core)
    started = []

    def begin(source, slot, device):
        made = copy(source, slot, device, len(started))
        made.start()
        started.append(made)

    for step in range(1, depth):
        begin(own, me, index(lax.rem(level + step, depth), side, core))
    begin(own, me, across)
    begin(own, me, partner)

    def arrived(slot):
        copy(out.at[slot], slot, partner, 0).wait_recv()

    def finish():
        for step in range(1, depth):
            slot = index(lax.rem(level - step + depth, depth), side, core)
            arrived(slot)
            begin(out.at[slot], slot, across)
            begin(out.at[slot], slot, partner)
        for step in range(depth):
            slot = index(lax.rem(level - step + depth, depth), 1 - side, core)
            arrived(slot)
            begin(out.at[slot], slot, partner)
        for step in range(depth):
            for b in range(2):
                arrived(index(lax.rem(level - step + depth, depth), b, 1 - core))
        for made in started:
            made.wait_send()

    return finish


def sends(n):
    depth = n // 4
    return 3 * depth - 1 + 2 * depth


def greet(n):
    me = lax.axis_index("row")
    barrier = pltpu.get_barrier_semaphore()
    for step in range(1, n):
        pl.semaphore_signal(
            barrier,
            inc=1,
            device_id={"row": lax.rem(me + step, n)},
            device_id_type=pl.DeviceIdType.MESH,
        )
    pl.semaphore_wait(barrier, n - 1)


def share_kernel(n, emi_ref, geo_ref, table_ref, out_ref, listed_ref, codes_ref, send, recv, list_send, list_recv):
    me = lax.axis_index("row")
    hours = emi_ref.shape[0]
    own_tiles = table_ref.shape[0] // n
    out_ref[me, :hours] = emi_ref[...]
    out_ref[me, hours : hours + 9] = geo_ref[...]
    out_ref[me, hours + 9 :] = jnp.zeros_like(out_ref[me, hours + 9 :])
    listed_ref[me] = table_ref[pl.ds(me * own_tiles, own_tiles)]
    greet(n)
    finish = start_gather(n, out_ref.at[me], out_ref, send, recv)
    lists = []
    for step in range(1, n):
        device = lax.rem(me + step, n)
        made = pltpu.make_async_remote_copy(
            src_ref=table_ref.at[pl.ds(device * own_tiles, own_tiles)],
            dst_ref=listed_ref.at[me],
            send_sem=list_send.at[step],
            recv_sem=list_recv.at[step],
            device_id={"row": device},
            device_id_type=pl.DeviceIdType.MESH,
        )
        made.start()
        lists.append(made)
    finish()
    for made in lists:
        made.wait()
    for d in range(n):
        codes_ref[d * own_tiles : (d + 1) * own_tiles, :] = listed_ref[d, :, 0, TILE:]


def field_kernel(n, field_ref, out_ref, send, recv):
    me = lax.axis_index("row")
    out_ref[me] = field_ref[...]
    greet(n)
    start_gather(n, field_ref, out_ref, send, recv)()


def split3(x):
    high = x.astype(jnp.bfloat16).astype(jnp.float32)
    rest = x - high
    mid = rest.astype(jnp.bfloat16).astype(jnp.float32)
    return high, mid, rest - mid


def split2(x):
    high = x.astype(jnp.bfloat16)
    return high, (x - high.astype(jnp.float32)).astype(jnp.bfloat16)


def frame(geo, center):
    corner = geo[0:3] - center
    u = geo[3:6]
    v = geo[6:9]
    ux, uy, uz = u[0:1], u[1:2], u[2:3]
    vx, vy, vz = v[0:1], v[1:2], v[2:3]
    cross = jnp.concatenate([uy * vz - uz * vy, uz * vx - ux * vz, ux * vy - uy * vx], axis=0)
    area = jnp.sqrt(jnp.sum(cross * cross, axis=0, keepdims=True))
    points = jnp.concatenate(
        [corner + s * u + t * v for s in (0.25, 0.75) for t in (0.25, 0.75)], axis=1
    )
    return points, corner, cross, area


def receiver_features(geo, center):
    points, corner, cross, area = frame(geo, center)
    normal = cross / area
    norms = jnp.sum(points * points, axis=0, keepdims=True)
    offset = -jnp.sum(normal * corner, axis=0, keepdims=True)
    wide = jnp.concatenate([-2.0 * points, normal], axis=1)
    fourth = jnp.concatenate([jnp.ones_like(norms), jnp.zeros_like(offset)], axis=1)
    fifth = jnp.concatenate([norms, offset], axis=1)
    rows = jnp.concatenate([wide, fourth, fifth, jnp.zeros((3, SPAN), jnp.float32)], axis=0)
    h, m, l = split3(rows)
    return jnp.concatenate([h, m, l, h, m, h], axis=0).astype(jnp.bfloat16)


def source_features(geo, center):
    points, corner, cross, area = frame(geo, center)
    scaled = cross * (1.0 / (16.0 * math.pi))
    norms = jnp.sum(points * points, axis=0, keepdims=True)
    spread = norms + jnp.concatenate([area * 0.25] * POINTS, axis=1)
    offset = -jnp.sum(scaled * corner, axis=0, keepdims=True)
    wide = jnp.concatenate([points, -0.5 * scaled], axis=1)
    fourth = jnp.concatenate([spread, offset], axis=1)
    fifth = jnp.concatenate([jnp.ones_like(norms), jnp.zeros_like(offset)], axis=1)
    rows = jnp.concatenate([wide, fourth, fifth, jnp.zeros((3, SPAN), jnp.float32)], axis=0)
    h, m, l = split3(rows)
    return jnp.concatenate([h, h, h, m, m, l], axis=0).T.astype(jnp.bfloat16)


def first_kernel(
    src_ref, packed, occ_ref, geo_own, emi_own, refl_ref,
    blocks_ref, field_ref, sums_ref, scale_ref,
    order, recv_feat, src_feat, dots, facing, total, acc, block, sent,
):
    own_tiles = geo_own.shape[1] // TILE
    slots = packed.shape[0] * own_tiles
    hours = emi_own.shape[0]
    center = jnp.mean(geo_own[0:3, :], axis=1, keepdims=True)

    def listing(k, live):
        order[live] = k
        return live + jnp.where(src_ref[k, 0] >= 0, 1, 0)

    count = lax.fori_loop(0, slots, listing, 0)
    for r in range(own_tiles):
        recv_feat[r] = receiver_features(geo_own[:, r * TILE : (r + 1) * TILE], center)
    acc[...] = jnp.zeros_like(acc)

    def place(slot):
        src = jnp.maximum(src_ref[slot, 0], 0)
        return slot // own_tiles, pl.ds(pl.multiple_of(src * TILE, TILE), TILE)

    def load_features(slot):
        d, where = place(slot)
        rows = source_features(packed[d, hours : hours + 9, where], center)
        for c in range(CHUNKS):
            for q in range(POINTS):
                src_feat[c * TILE + q * PART : c * TILE + (q + 1) * PART, :] = rows[
                    q * TILE + c * PART : q * TILE + (c + 1) * PART
                ]
        src_feat[POINTS * TILE :, :] = rows[POINTS * TILE :]

    def product(r, piece, start, wide):
        return jnp.dot(
            src_feat[piece * TILE : (piece + 1) * TILE, :],
            recv_feat[r, :, start : start + wide],
            preferred_element_type=jnp.float32,
        )

    def face(r, c):
        facing[c * TILE : (c + 1) * TILE, :] = jnp.maximum(
            product(r, c, POINTS * TILE, TILE), 0.0
        )

    def fill(r, c, half):
        dots[half, c * TILE : (c + 1) * TILE, :] = product(r, c, half * WIDE, WIDE)

    def combine(half, c, finish):
        for b in range(PART // BAND):
            inner = b * BAND
            parts = [jnp.zeros((BAND, TILE), jnp.float32) for _ in range(WIDE // TILE)]
            for q in range(POINTS):
                row = c * TILE + q * PART + inner
                ahead = facing[row : row + BAND, :]
                for k in range(WIDE // TILE):
                    spread = dots[half, row : row + BAND, k * TILE : (k + 1) * TILE]
                    parts[k] += ahead * pl.reciprocal(spread * spread, approx=True)
            row = c * PART + inner
            value = None
            for k in range(WIDE // TILE):
                start = POINTS * TILE + row
                back = dots[half, start : start + BAND, k * TILE : (k + 1) * TILE]
                term = jnp.maximum(back, 0.0) * parts[k]
                value = term if value is None else value + term
            if half == 0:
                total[row : row + BAND, :] = value
            else:
                finish(row, total[row : row + BAND, :] + value)

    def prepare(slot):
        load_features(slot)
        r = lax.rem(slot, own_tiles)
        fill(r, CHUNKS, 0)
        for c in range(CHUNKS):
            face(r, c)
            fill(r, c, 0)

    def stored(slot, spot):
        return pltpu.make_async_copy(block.at[spot], blocks_ref.at[slot], sent.at[spot])

    prepare(order[0])

    def one(i, carry):
        slot = order[i]
        later = order[jnp.minimum(i + 1, count - 1)]
        r = lax.rem(slot, own_tiles)
        later_r = lax.rem(later, own_tiles)
        d, where = place(slot)
        words = occ_ref[d, r, :, :TILE]
        spot = lax.rem(i, 2)

        @pl.when(i >= 2)
        def _():
            stored(slot, spot).wait()

        def finish(row, value):
            bit = jnp.bitwise_and(jnp.right_shift(words, row // BAND), 1).astype(jnp.float32)
            high, low = split2(value * bit)
            block[spot, row : row + BAND, :] = high
            block[spot, TILE + row : TILE + row + BAND, :] = low

        fill(r, CHUNKS, 1)
        for c in range(CHUNKS):
            fill(r, c, 1)
            combine(0, c, finish)
        load_features(later)
        fill(later_r, CHUNKS, 0)
        for c in range(CHUNKS):
            combine(1, c, finish)
            face(later_r, c)
            fill(later_r, c, 0)
        stored(slot, spot).start()
        high, low = split2(packed[d, :hours, where])
        left = jnp.concatenate([high, low, jnp.ones_like(high)], axis=0)
        acc[r] += jnp.dot(
            jnp.concatenate([left, left], axis=1),
            block[spot],
            preferred_element_type=jnp.float32,
        )
        return carry

    lax.fori_loop(0, count, one, 0)
    for spot in range(2):

        @pl.when(count > spot)
        def _():
            stored(0, spot).wait()

    for r in range(own_tiles):
        lanes = slice(r * TILE, (r + 1) * TILE)
        sums = acc[r, 2 * hours : 2 * hours + 1, :]
        irr = acc[r, 0:hours, :] + acc[r, hours : 2 * hours, :]
        scale = refl_ref[:, lanes] / jnp.maximum(sums, 1.0)
        sums_ref[:, lanes] = sums
        scale_ref[:, lanes] = scale
        field_ref[:, lanes] = emi_own[:, lanes] + scale * irr


def later_kernel(src_ref, blocks_ref, field_all, emi_own, scale_ref, out_ref, acc, held, arrived):
    slots = field_all.shape[0]
    own_tiles = emi_own.shape[1] // TILE
    hours = emi_own.shape[0]

    def fetch(slot):
        return pltpu.make_async_copy(blocks_ref.at[slot], held.at[slot], arrived.at[slot])

    for r in range(own_tiles):

        def begin(d, carry):
            slot = d * own_tiles + r

            @pl.when(src_ref[slot, 0] >= 0)
            def _():
                fetch(slot).start()

            return carry

        lax.fori_loop(0, slots, begin, 0)

    for r in range(own_tiles):
        lanes = slice(r * TILE, (r + 1) * TILE)
        acc[...] = jnp.zeros_like(acc)

        def one(d, carry):
            slot = d * own_tiles + r
            src = src_ref[slot, 0]

            @pl.when(src >= 0)
            def _():
                where = pl.ds(pl.multiple_of(src * TILE, TILE), TILE)
                high, low = split2(field_all[d, :, where])
                left = jnp.concatenate([high, low], axis=0)
                fetch(slot).wait()
                acc[...] += jnp.dot(
                    jnp.concatenate([left, left], axis=1),
                    held[slot],
                    preferred_element_type=jnp.float32,
                )

            return carry

        lax.fori_loop(0, slots, one, 0)
        irr = acc[0:hours, :] + acc[hours : 2 * hours, :]
        out_ref[:, lanes] = emi_own[:, lanes] + scale_ref[:, lanes] * irr


def on_device(n, geometry, emission, reflect, occlusion, pair_recv, pair_src, pair_count):
    width = geometry.shape[1]
    hours = emission.shape[0]
    own_tiles = width // TILE
    tiles = own_tiles * n
    f32 = jnp.float32
    limit = pltpu.CompilerParams(vmem_limit_bytes=60 * 1024 * 1024)

    table = pl.pallas_call(
        sort_kernel,
        out_shape=jax.ShapeDtypeStruct((tiles, 1, TILE + 128), jnp.int32),
        in_specs=[SMEM, SMEM, SMEM, VMEM],
        out_specs=VMEM,
    )(pair_recv, pair_src, pair_count, occlusion)
    dma = pltpu.SemaphoreType.DMA
    packed, listed, codes = pl.pallas_call(
        functools.partial(share_kernel, n),
        out_shape=(
            jax.ShapeDtypeStruct((n, PACK, width), f32),
            jax.ShapeDtypeStruct((n, own_tiles, 1, TILE + 128), jnp.int32),
            jax.ShapeDtypeStruct((tiles, 128), jnp.int32),
        ),
        in_specs=[VMEM] * 3,
        out_specs=(VMEM,) * 3,
        scratch_shapes=[dma((sends(n),)), dma((n,)), dma((n,)), dma((n,))],
        compiler_params=pltpu.CompilerParams(
            collective_id=0, has_side_effects=True, vmem_limit_bytes=60 * 1024 * 1024
        ),
    )(emission, geometry, table)

    blocks, field, sums, scale = pl.pallas_call(
        first_kernel,
        out_shape=(
            jax.ShapeDtypeStruct((tiles, 2 * TILE, TILE), jnp.bfloat16),
            jax.ShapeDtypeStruct((hours, width), f32),
            jax.ShapeDtypeStruct((1, width), f32),
            jax.ShapeDtypeStruct((1, width), f32),
        ),
        in_specs=[SMEM] + [VMEM] * 5,
        out_specs=(ANY,) + (VMEM,) * 3,
        scratch_shapes=[
            pltpu.SMEM((tiles,), jnp.int32),
            pltpu.VMEM((own_tiles, FEATS, SPAN), jnp.bfloat16),
            pltpu.VMEM((SPAN, FEATS), jnp.bfloat16),
            pltpu.VMEM((2, SPAN, WIDE), f32),
            pltpu.VMEM((POINTS * TILE, TILE), f32),
            pltpu.VMEM((TILE, TILE), f32),
            pltpu.VMEM((own_tiles, 3 * hours, TILE), f32),
            pltpu.VMEM((2, 2 * TILE, TILE), jnp.bfloat16),
            dma((2,)),
        ],
        compiler_params=limit,
    )(codes, packed, listed, geometry, emission, reflect.reshape(1, width))

    field_all = pl.pallas_call(
        functools.partial(field_kernel, n),
        out_shape=jax.ShapeDtypeStruct((n, hours, width), f32),
        in_specs=[VMEM],
        out_specs=VMEM,
        scratch_shapes=[dma((sends(n),)), dma((n,))],
        compiler_params=pltpu.CompilerParams(
            collective_id=1, has_side_effects=True, vmem_limit_bytes=60 * 1024 * 1024
        ),
    )(field)
    radiosity = pl.pallas_call(
        later_kernel,
        out_shape=jax.ShapeDtypeStruct((hours, width), f32),
        in_specs=[SMEM, ANY] + [VMEM] * 3,
        out_specs=VMEM,
        scratch_shapes=[
            pltpu.VMEM((2 * hours, TILE), f32),
            pltpu.VMEM((tiles, 2 * TILE, TILE), jnp.bfloat16),
            dma((tiles,)),
        ],
        compiler_params=limit,
    )(codes, blocks, field_all, emission, scale)
    return (radiosity, sums.reshape(width))


def solution(mesh):
    placed = (
        P(None, ("grp", "row")),
        P(None, ("grp", "row")),
        P(("grp", "row")),
        P(("grp", "row"), None),
        P(("grp", "row")),
        P(("grp", "row")),
        P(("grp", "row")),
    )
    return jax.shard_map(
        functools.partial(on_device, mesh.shape["row"]),
        mesh=mesh,
        in_specs=placed,
        out_specs=(P(None, ("grp", "row")), P(("grp", "row"))),
        check_vma=False,
    )
```

```python
import functools
import math

import jax
import jax.numpy as jnp
from jax import lax
from jax.experimental import pallas as pl
from jax.experimental.pallas import tpu as pltpu
from jax.sharding import PartitionSpec as P

TILE = 256
GROUPS = 16
BAND = TILE // GROUPS
POINTS = 4
FEATS = 48
LANES = 128
CHUNKS = 4
PART = TILE // CHUNKS
WIDE = 2 * TILE
SPAN = (POINTS + 1) * TILE
VMEM = pl.BlockSpec(memory_space=pltpu.VMEM)
ANY = pl.BlockSpec(memory_space=pl.ANY)
SMEM = pl.BlockSpec(memory_space=pltpu.SMEM)


def sort_kernel(recv_ref, src_ref, count_ref, occ_ref, table_ref):
    tiles = table_ref.shape[0]
    table_ref[:, :, :TILE] = jnp.zeros((tiles, 1, TILE), jnp.int32)
    table_ref[:, :, TILE:] = jnp.full((tiles, 1, 128), -1, jnp.int32)

    def place(k, carry):
        row = recv_ref[k]
        table_ref[row, :, :TILE] = occ_ref[pl.ds(k, 1), :]
        table_ref[row, :, TILE:] = jnp.full((1, 128), src_ref[k], jnp.int32)
        return carry

    lax.fori_loop(0, count_ref[0], place, 0)


def start_gather(n, own, out, send, recv):
    me = lax.axis_index("row")
    depth = n // 4
    core = lax.rem(me, 2)
    side = lax.rem(me // 2, 2)
    level = me // 4

    def index(a, b, c):
        return a * 4 + b * 2 + c

    def copy(source, slot, device, k):
        return pltpu.make_async_remote_copy(
            src_ref=source,
            dst_ref=out.at[slot],
            send_sem=send.at[k],
            recv_sem=recv.at[slot],
            device_id={"row": device},
            device_id_type=pl.DeviceIdType.MESH,
        )

    across = index(level, 1 - side, core)
    partner = index(level, side, 1 - core)
    started = []

    def begin(source, slot, device):
        made = copy(source, slot, device, len(started))
        made.start()
        started.append(made)

    for step in range(1, depth):
        begin(own, me, index(lax.rem(level + step, depth), side, core))
    begin(own, me, across)
    begin(own, me, partner)

    def arrived(slot):
        copy(out.at[slot], slot, partner, 0).wait_recv()

    def finish():
        for step in range(1, depth):
            slot = index(lax.rem(level - step + depth, depth), side, core)
            arrived(slot)
            begin(out.at[slot], slot, across)
            begin(out.at[slot], slot, partner)
        for step in range(depth):
            slot = index(lax.rem(level - step + depth, depth), 1 - side, core)
            arrived(slot)
            begin(out.at[slot], slot, partner)
        for step in range(depth):
            for b in range(2):
                arrived(index(lax.rem(level - step + depth, depth), b, 1 - core))
        for made in started:
            made.wait_send()

    return finish


def sends(n):
    depth = n // 4
    return 3 * depth - 1 + 2 * depth


def greet(devices):
    barrier = pltpu.get_barrier_semaphore()
    for device in devices:
        pl.semaphore_signal(
            barrier,
            inc=1,
            device_id={"row": device},
            device_id_type=pl.DeviceIdType.MESH,
        )
    pl.semaphore_wait(barrier, len(devices))


def share_kernel(n, emi_ref, geo_ref, table_ref, out_ref, listed_ref, codes_ref, send, recv, list_send, list_recv):
    me = lax.axis_index("row")
    hours = emi_ref.shape[0]
    own_tiles = table_ref.shape[0] // n
    blocks = emi_ref.shape[1] // LANES
    for k in range(blocks):
        lanes = slice(k * LANES, (k + 1) * LANES)
        out_ref[me, k * hours : (k + 1) * hours] = emi_ref[:, lanes]
        row = blocks * hours + k * 8
        out_ref[me, row : row + 8] = geo_ref[0:8, lanes]
        row = blocks * (hours + 8) + k
        out_ref[me, row : row + 1] = geo_ref[8:9, lanes]
    used = blocks * (hours + 9)
    if used < out_ref.shape[1]:
        out_ref[me, used:] = jnp.zeros((out_ref.shape[1] - used, LANES), jnp.float32)
    listed_ref[me] = table_ref[pl.ds(me * own_tiles, own_tiles)]
    greet([lax.rem(me + step, n) for step in range(1, n)])
    finish = start_gather(n, out_ref.at[me], out_ref, send, recv)
    lists = []
    for step in range(1, n):
        device = lax.rem(me + step, n)
        made = pltpu.make_async_remote_copy(
            src_ref=table_ref.at[pl.ds(device * own_tiles, own_tiles)],
            dst_ref=listed_ref.at[me],
            send_sem=list_send.at[step],
            recv_sem=list_recv.at[step],
            device_id={"row": device},
            device_id_type=pl.DeviceIdType.MESH,
        )
        made.start()
        lists.append(made)
    finish()
    for made in lists:
        made.wait()
    for d in range(n):
        codes_ref[d * own_tiles : (d + 1) * own_tiles, :] = listed_ref[d, :, 0, TILE:]


def field_kernel(n, field_ref, out_ref, send, recv):
    me = lax.axis_index("row")
    out_ref[me] = field_ref[...]
    core = lax.rem(me, 2)
    side = lax.rem(me // 2, 2)
    greet(
        [lax.rem(me + 4 * step, n) for step in range(1, n // 4)]
        + [me + 2 - 4 * side, me + 1 - 2 * core]
    )
    start_gather(n, field_ref, out_ref, send, recv)()


def split3(x):
    high = x.astype(jnp.bfloat16).astype(jnp.float32)
    rest = x - high
    mid = rest.astype(jnp.bfloat16).astype(jnp.float32)
    return high, mid, rest - mid


def split2(x):
    high = x.astype(jnp.bfloat16)
    return high, (x - high.astype(jnp.float32)).astype(jnp.bfloat16)


def frame(geo, center):
    corner = geo[0:3] - center
    u = geo[3:6]
    v = geo[6:9]
    ux, uy, uz = u[0:1], u[1:2], u[2:3]
    vx, vy, vz = v[0:1], v[1:2], v[2:3]
    cross = jnp.concatenate([uy * vz - uz * vy, uz * vx - ux * vz, ux * vy - uy * vx], axis=0)
    area = jnp.sqrt(jnp.sum(cross * cross, axis=0, keepdims=True))
    points = jnp.concatenate(
        [corner + s * u + t * v for s in (0.25, 0.75) for t in (0.25, 0.75)], axis=1
    )
    return points, corner, cross, area


def receiver_features(geo, center):
    points, corner, cross, area = frame(geo, center)
    normal = cross / area
    norms = jnp.sum(points * points, axis=0, keepdims=True)
    offset = -jnp.sum(normal * corner, axis=0, keepdims=True)
    wide = jnp.concatenate([-2.0 * points, normal], axis=1)
    fourth = jnp.concatenate([jnp.ones_like(norms), jnp.zeros_like(offset)], axis=1)
    fifth = jnp.concatenate([norms, offset], axis=1)
    rows = jnp.concatenate([wide, fourth, fifth, jnp.zeros((3, SPAN), jnp.float32)], axis=0)
    h, m, l = split3(rows)
    return jnp.concatenate([h, m, l, h, m, h], axis=0).astype(jnp.bfloat16)


def source_features(geo, center):
    points, corner, cross, area = frame(geo, center)
    scaled = cross * (1.0 / (16.0 * math.pi))
    norms = jnp.sum(points * points, axis=0, keepdims=True)
    spread = norms + jnp.concatenate([area * 0.25] * POINTS, axis=1)
    offset = -jnp.sum(scaled * corner, axis=0, keepdims=True)
    wide = jnp.concatenate([points, -0.5 * scaled], axis=1)
    fourth = jnp.concatenate([spread, offset], axis=1)
    fifth = jnp.concatenate([jnp.ones_like(norms), jnp.zeros_like(offset)], axis=1)
    rows = jnp.concatenate([wide, fourth, fifth, jnp.zeros((3, SPAN), jnp.float32)], axis=0)
    h, m, l = split3(rows)
    return jnp.concatenate([h, h, h, m, m, l], axis=0).T.astype(jnp.bfloat16)


def first_kernel(
    src_ref, packed, occ_ref, geo_own, emi_own, refl_ref,
    blocks_ref, field_ref, sums_ref, scale_ref,
    order, recv_feat, src_feat, dots, facing, total, acc, block, sent,
):
    own_tiles = geo_own.shape[1] // TILE
    slots = packed.shape[0] * own_tiles
    hours = emi_own.shape[0]
    blocks = geo_own.shape[1] // LANES
    center = jnp.mean(geo_own[0:3, :], axis=1, keepdims=True)

    def listing(k, live):
        order[live] = k
        return live + jnp.where(src_ref[k, 0] >= 0, 1, 0)

    count = lax.fori_loop(0, slots, listing, 0)
    for r in range(own_tiles):
        recv_feat[r] = receiver_features(geo_own[:, r * TILE : (r + 1) * TILE], center)
    acc[...] = jnp.zeros_like(acc)

    def place(slot):
        return slot // own_tiles, jnp.maximum(src_ref[slot, 0], 0) * (TILE // LANES)

    def emission_of(d, first):
        rows = [pl.multiple_of((first + k) * hours, 8) for k in range(TILE // LANES)]
        return jnp.concatenate([packed[d, pl.ds(row, hours), :] for row in rows], axis=1)

    def geometry_of(d, first):
        halves = []
        for k in range(TILE // LANES):
            row = pl.multiple_of(blocks * hours + (first + k) * 8, 8)
            last = blocks * (hours + 8) + first + k
            halves.append(
                jnp.concatenate(
                    [packed[d, pl.ds(row, 8), :], packed[d, pl.ds(last, 1), :]], axis=0
                )
            )
        return jnp.concatenate(halves, axis=1)

    def load_features(slot):
        d, first = place(slot)
        rows = source_features(geometry_of(d, first), center)
        for c in range(CHUNKS):
            for q in range(POINTS):
                src_feat[c * TILE + q * PART : c * TILE + (q + 1) * PART, :] = rows[
                    q * TILE + c * PART : q * TILE + (c + 1) * PART
                ]
        src_feat[POINTS * TILE :, :] = rows[POINTS * TILE :]

    def product(r, piece, start, wide):
        return jnp.dot(
            src_feat[piece * TILE : (piece + 1) * TILE, :],
            recv_feat[r, :, start : start + wide],
            preferred_element_type=jnp.float32,
        )

    def face(r, c):
        facing[c * TILE : (c + 1) * TILE, :] = jnp.maximum(
            product(r, c, POINTS * TILE, TILE), 0.0
        )

    def fill(r, c, half):
        dots[half, c * TILE : (c + 1) * TILE, :] = product(r, c, half * WIDE, WIDE)

    def combine(half, c, finish):
        for b in range(PART // BAND):
            inner = b * BAND
            parts = [jnp.zeros((BAND, TILE), jnp.float32) for _ in range(WIDE // TILE)]
            for q in range(POINTS):
                row = c * TILE + q * PART + inner
                ahead = facing[row : row + BAND, :]
                for k in range(WIDE // TILE):
                    spread = dots[half, row : row + BAND, k * TILE : (k + 1) * TILE]
                    parts[k] += ahead * pl.reciprocal(spread * spread, approx=True)
            row = c * PART + inner
            value = None
            for k in range(WIDE // TILE):
                start = POINTS * TILE + row
                back = dots[half, start : start + BAND, k * TILE : (k + 1) * TILE]
                term = jnp.maximum(back, 0.0) * parts[k]
                value = term if value is None else value + term
            if half == 0:
                total[row : row + BAND, :] = value
            else:
                finish(row, total[row : row + BAND, :] + value)

    def prepare(slot):
        load_features(slot)
        r = lax.rem(slot, own_tiles)
        fill(r, CHUNKS, 0)
        for c in range(CHUNKS):
            face(r, c)
            fill(r, c, 0)

    def stored(slot, spot):
        return pltpu.make_async_copy(block.at[spot], blocks_ref.at[slot], sent.at[spot])

    prepare(order[0])

    def one(i, carry):
        slot = order[i]
        later = order[jnp.minimum(i + 1, count - 1)]
        r = lax.rem(slot, own_tiles)
        later_r = lax.rem(later, own_tiles)
        d, first = place(slot)
        words = occ_ref[d, r, :, :TILE]
        spot = lax.rem(i, 2)

        @pl.when(i >= 2)
        def _():
            stored(slot, spot).wait()

        def finish(row, value):
            bit = jnp.bitwise_and(jnp.right_shift(words, row // BAND), 1).astype(jnp.float32)
            high, low = split2(value * bit)
            block[spot, row : row + BAND, :] = high
            block[spot, TILE + row : TILE + row + BAND, :] = low

        fill(r, CHUNKS, 1)
        for c in range(CHUNKS):
            fill(r, c, 1)
            combine(0, c, finish)
        load_features(later)
        fill(later_r, CHUNKS, 0)
        for c in range(CHUNKS):
            combine(1, c, finish)
            face(later_r, c)
            fill(later_r, c, 0)
        stored(slot, spot).start()
        high, low = split2(emission_of(d, first))
        left = jnp.concatenate([high, low, jnp.ones_like(high)], axis=0)
        acc[r] += jnp.dot(
            jnp.concatenate([left, left], axis=1),
            block[spot],
            preferred_element_type=jnp.float32,
        )
        return carry

    lax.fori_loop(0, count, one, 0)
    for spot in range(2):

        @pl.when(count > spot)
        def _():
            stored(0, spot).wait()

    for r in range(own_tiles):
        lanes = slice(r * TILE, (r + 1) * TILE)
        sums = acc[r, 2 * hours : 2 * hours + 1, :]
        irr = acc[r, 0:hours, :] + acc[r, hours : 2 * hours, :]
        scale = refl_ref[:, lanes] / jnp.maximum(sums, 1.0)
        sums_ref[:, lanes] = sums
        scale_ref[:, lanes] = scale
        field_ref[:, lanes] = emi_own[:, lanes] + scale * irr


def later_kernel(src_ref, blocks_ref, field_all, emi_own, scale_ref, out_ref, acc, held, arrived):
    slots = field_all.shape[0]
    own_tiles = emi_own.shape[1] // TILE
    hours = emi_own.shape[0]

    def fetch(slot):
        return pltpu.make_async_copy(blocks_ref.at[slot], held.at[slot], arrived.at[slot])

    for r in range(own_tiles):

        def begin(d, carry):
            slot = d * own_tiles + r

            @pl.when(src_ref[slot, 0] >= 0)
            def _():
                fetch(slot).start()

            return carry

        lax.fori_loop(0, slots, begin, 0)

    for r in range(own_tiles):
        lanes = slice(r * TILE, (r + 1) * TILE)
        acc[...] = jnp.zeros_like(acc)

        def one(d, carry):
            slot = d * own_tiles + r
            src = src_ref[slot, 0]

            @pl.when(src >= 0)
            def _():
                where = pl.ds(pl.multiple_of(src * TILE, TILE), TILE)
                high, low = split2(field_all[d, :, where])
                left = jnp.concatenate([high, low], axis=0)
                fetch(slot).wait()
                acc[...] += jnp.dot(
                    jnp.concatenate([left, left], axis=1),
                    held[slot],
                    preferred_element_type=jnp.float32,
                )

            return carry

        lax.fori_loop(0, slots, one, 0)
        irr = acc[0:hours, :] + acc[hours : 2 * hours, :]
        out_ref[:, lanes] = emi_own[:, lanes] + scale_ref[:, lanes] * irr


def on_device(n, geometry, emission, reflect, occlusion, pair_recv, pair_src, pair_count):
    width = geometry.shape[1]
    hours = emission.shape[0]
    own_tiles = width // TILE
    tiles = own_tiles * n
    f32 = jnp.float32
    limit = pltpu.CompilerParams(vmem_limit_bytes=60 * 1024 * 1024)

    table = pl.pallas_call(
        sort_kernel,
        out_shape=jax.ShapeDtypeStruct((tiles, 1, TILE + 128), jnp.int32),
        in_specs=[SMEM, SMEM, SMEM, VMEM],
        out_specs=VMEM,
    )(pair_recv, pair_src, pair_count, occlusion)
    dma = pltpu.SemaphoreType.DMA
    packed, listed, codes = pl.pallas_call(
        functools.partial(share_kernel, n),
        out_shape=(
            jax.ShapeDtypeStruct((n, -(-(width // LANES) * (hours + 9) // 8) * 8, LANES), f32),
            jax.ShapeDtypeStruct((n, own_tiles, 1, TILE + 128), jnp.int32),
            jax.ShapeDtypeStruct((tiles, 128), jnp.int32),
        ),
        in_specs=[VMEM] * 3,
        out_specs=(VMEM,) * 3,
        scratch_shapes=[dma((sends(n),)), dma((n,)), dma((n,)), dma((n,))],
        compiler_params=pltpu.CompilerParams(
            collective_id=0, has_side_effects=True, vmem_limit_bytes=60 * 1024 * 1024
        ),
    )(emission, geometry, table)

    blocks, field, sums, scale = pl.pallas_call(
        first_kernel,
        out_shape=(
            jax.ShapeDtypeStruct((tiles, 2 * TILE, TILE), jnp.bfloat16),
            jax.ShapeDtypeStruct((hours, width), f32),
            jax.ShapeDtypeStruct((1, width), f32),
            jax.ShapeDtypeStruct((1, width), f32),
        ),
        in_specs=[SMEM] + [VMEM] * 5,
        out_specs=(ANY,) + (VMEM,) * 3,
        scratch_shapes=[
            pltpu.SMEM((tiles,), jnp.int32),
            pltpu.VMEM((own_tiles, FEATS, SPAN), jnp.bfloat16),
            pltpu.VMEM((SPAN, FEATS), jnp.bfloat16),
            pltpu.VMEM((2, SPAN, WIDE), f32),
            pltpu.VMEM((POINTS * TILE, TILE), f32),
            pltpu.VMEM((TILE, TILE), f32),
            pltpu.VMEM((own_tiles, 3 * hours, TILE), f32),
            pltpu.VMEM((2, 2 * TILE, TILE), jnp.bfloat16),
            dma((2,)),
        ],
        compiler_params=limit,
    )(codes, packed, listed, geometry, emission, reflect.reshape(1, width))

    field_all = pl.pallas_call(
        functools.partial(field_kernel, n),
        out_shape=jax.ShapeDtypeStruct((n, hours, width), f32),
        in_specs=[VMEM],
        out_specs=VMEM,
        scratch_shapes=[dma((sends(n),)), dma((n,))],
        compiler_params=pltpu.CompilerParams(
            collective_id=1, has_side_effects=True, vmem_limit_bytes=60 * 1024 * 1024
        ),
    )(field)
    radiosity = pl.pallas_call(
        later_kernel,
        out_shape=jax.ShapeDtypeStruct((hours, width), f32),
        in_specs=[SMEM, ANY] + [VMEM] * 3,
        out_specs=VMEM,
        scratch_shapes=[
            pltpu.VMEM((2 * hours, TILE), f32),
            pltpu.VMEM((tiles, 2 * TILE, TILE), jnp.bfloat16),
            dma((tiles,)),
        ],
        compiler_params=limit,
    )(codes, blocks, field_all, emission, scale)
    return (radiosity, sums.reshape(width))


def solution(mesh):
    placed = (
        P(None, ("grp", "row")),
        P(None, ("grp", "row")),
        P(("grp", "row")),
        P(("grp", "row"), None),
        P(("grp", "row")),
        P(("grp", "row")),
        P(("grp", "row")),
    )
    return jax.shard_map(
        functools.partial(on_device, mesh.shape["row"]),
        mesh=mesh,
        in_specs=placed,
        out_specs=(P(None, ("grp", "row")), P(("grp", "row"))),
        check_vma=False,
    )
```
